32 devices in a mesh: groups: 2 (over y), seq: 4 (over z), head: 2 (over x), sub: 2 (over core).
Axes of the slice: x: 2, y: 2, z: 4, core: 2. Of those that a mesh axis runs over, the one named last changes fastest.
Arguments:
- queries: bfloat16 [6144, 3072], P(('groups', 'seq', 'sub'), 'head'), parts along dimension 0, may hold values from -6 to 6
- keys: bfloat16 [6144, 3072], P(('groups', 'seq', 'sub'), 'head'), parts along dimension 0, may hold values from -6 to 6
- values: bfloat16 [6144, 3072], P(('groups', 'seq', 'sub'), 'head'), parts along dimension 0, may hold values from -6 to 6
- kv_list: int32 [16, 6], P(('groups', 'seq', 'sub')), parts along dimension 0, may hold values from -1 to 7, as said below
- kv_count: int32 [16], P(('groups', 'seq', 'sub')), parts along dimension 0, may hold values from 1 to 6, as said below
- out_weight: bfloat16 [3072, 3072], P('head'), may hold values from -0.5 to 0.5
- gate: float32 [3072], P('head'), may hold values from 1 to 4
Outputs:
- layer_out: bfloat16 [6144, 3072], P(('groups', 'seq', 'sub'), 'head'), parts along dimension 0
The draws below stay inside these ranges and needn't reach their ends.
There are 2 independent parts, one for each index of `groups`. The reference program is written for one: setup_inputs(seed, part) draws one part's arguments, and reference() takes and returns one part's arrays. A program takes and returns all parts, laid end to end along the dimension named above; an argument that names none is the same for every part. Nothing has to cross between parts.
Inputs may be any that keep to these rules, and one draw needn't show every extreme that they name: `kv_list`: tile t lies at time t // 2 and height t % 2 of a slab of 4 x 2 x 1 tiles. Row t begins with t itself, then lists in a drawn order the other tiles of t's 3 x 3 x 3 window clipped to the slab (time within one of t's), then -1 in the entries left over. `kv_count`: at most the number of tiles in the row's clipped window; some tile has 6 and some tile has 1.
All inputs are finite; a program needn't handle non-finite values.
Results may differ from the reference program's by a relative error of at most 0.014.
Values may be sent and summed in bfloat16 or wider, within the bound.
A program may use at most 128 MiB of HBM per device.

```python
import math
import jax
import jax.numpy as jnp
from jax import lax

HEADS = 24
HD = 128
D = 3072
TILE = 384
WIN = 6
TILES = 8
TOKENS = 3072
N_HEAD = 2


def drawn_field(key, which_one):
    shape = (TILES, TILE, HEADS * HD)
    field = jnp.clip(1.5 * jax.random.normal(jax.random.fold_in(key, 11 + which_one), shape, jnp.float32), -6.0, 6.0)
    return field.reshape(TOKENS, HEADS * HD).astype(jnp.bfloat16)


def draw_queries(key, part):
    return drawn_field(key, 0)


def draw_keys(key, part):
    return drawn_field(key, 1)


def window_lists(key):
    tile_ids = jnp.arange(TILES, dtype=jnp.int32)
    times = tile_ids // 2
    eligible = (jnp.abs(times[:, None] - times[None, :]) <= 1) & (tile_ids[:, None] != tile_ids[None, :])
    noise = jax.random.randint(jax.random.fold_in(key, 31), (TILES, TILES), 0, 65536)
    ranking = jnp.where(eligible, noise * TILES + tile_ids[None, :] + 1, 0)
    scored, picked = lax.top_k(ranking, WIN - 1)
    others = jnp.where(scored > 0, picked.astype(jnp.int32), -1)
    lists = jnp.concatenate([tile_ids[:, None], others], axis=1)
    window_size = 1 + jnp.sum(eligible.astype(jnp.int32), axis=1)
    raw_drops = jax.random.randint(jax.random.fold_in(key, 32), (TILES,), 0, 65536)
    counts = window_size - raw_drops % (window_size // 2 + 1)
    busiest = jax.random.randint(jax.random.fold_in(key, 34), (), 2, TILES - 2)
    corner = jax.random.randint(jax.random.fold_in(key, 35), (), 0, 4)
    lonely = jnp.where(corner < 2, corner, TILES - 4 + corner)
    counts = jnp.where(tile_ids == busiest, WIN, counts)
    counts = jnp.where(tile_ids == lonely, 1, counts)
    return (lists.astype(jnp.int32), counts.astype(jnp.int32))


def draw_kv_list(key, part):
    return window_lists(key)[0]


def draw_kv_count(key, part):
    return window_lists(key)[1]


def block_levels(key, dims, shards, smallest, largest):
    def one(dim, blocks):
        heights = jax.random.uniform(jax.random.fold_in(jax.random.fold_in(key, 6), dim), (blocks,), jnp.float32, smallest / len(shards), largest / len(shards))
        return jnp.repeat(jnp.exp(heights), dims[dim] // blocks).reshape((-1,) + (1,) * (len(dims) - dim - 1))

    level = one(*shards[0])
    for cut in shards[1:]:
        level = level * one(*cut)
    return level


def normal_values(stream_key, shape, spread, bound, pieces=(), held_as=jnp.bfloat16):
    level = block_levels(stream_key, shape, pieces, -0.22, 0.18) if pieces else 1.0
    values = jax.random.normal(stream_key, shape, jnp.float32) * spread * level
    return jnp.minimum(jnp.maximum(values, -bound), bound).astype(held_as)


def setup_inputs(seed: int = 0, part: int = 0) -> dict:
    arg_keys = jax.random.split(jax.random.key(seed), 8)
    part_keys = jax.random.split(jax.random.fold_in(arg_keys[7], part), 8)
    return {
        "queries": draw_queries(jax.random.fold_in(jax.random.fold_in(arg_keys[7], part), 71), part),
        "keys": draw_keys(jax.random.fold_in(jax.random.fold_in(arg_keys[7], part), 71), part),
        "values": normal_values(part_keys[2], (TOKENS, D), 1.0, 6.0, ((0, 8), (1, 2))),
        "kv_list": draw_kv_list(jax.random.fold_in(jax.random.fold_in(arg_keys[7], part), 71), part),
        "kv_count": draw_kv_count(jax.random.fold_in(jax.random.fold_in(arg_keys[7], part), 71), part),
        "out_weight": normal_values(arg_keys[5], (D, D), HD ** -0.5, 0.5, ((0, 2),)),
        "gate": jnp.clip(jnp.exp(math.log(4.0) - 1.3862944 * jax.random.uniform(arg_keys[6], (D,), jnp.float32) ** block_levels(arg_keys[6], (D,), ((0, 2),), -0.2, 0.2)), 1.0, 4.0),
    }


NEG_FILL = -1e+30

def reference(queries, keys, values, kv_list, kv_count, out_weight, gate):
    heads_all = queries.shape[1] // HD
    query_tiles = queries.reshape(TILES, TILE, heads_all, HD)
    key_tiles = keys.reshape(TILES, TILE, heads_all, HD)
    value_tiles = values.reshape(TILES, TILE, heads_all, HD)
    score_scale = 1.0 / math.sqrt(HD)

    def one_tile(tile_index):
        listed = jnp.maximum(kv_list[tile_index], 0).astype(jnp.int32)
        near_keys = key_tiles[listed].astype(jnp.float32)
        near_values = value_tiles[listed].astype(jnp.float32)
        live = jnp.arange(WIN) < kv_count[tile_index]
        scores = jnp.einsum('qhd,wkhd->hqwk', query_tiles[tile_index].astype(jnp.float32), near_keys) * score_scale
        scores = jnp.where(live[None, None, :, None], scores, NEG_FILL)
        peak = lax.optimization_barrier(jnp.max(scores, axis=(2, 3), keepdims=True))
        weights = jnp.exp(scores - peak)
        total = lax.optimization_barrier(jnp.sum(weights, axis=(2, 3)))
        rounded = lax.optimization_barrier(weights.astype(jnp.bfloat16)).astype(jnp.float32)
        mixed = jnp.einsum('hqwk,wkhd->qhd', rounded, near_values)
        return (mixed / jnp.transpose(total)[:, :, None]).astype(jnp.bfloat16)
    attention = lax.map(one_tile, jnp.arange(TILES)).reshape(TOKENS, D)
    group_width = D // N_HEAD
    grouped = attention.reshape(TOKENS, N_HEAD, group_width)
    weight_groups = out_weight.reshape(N_HEAD, group_width, D)

    def add_group(summed, group_index):
        partial_term = jnp.dot(grouped[:, group_index, :], weight_groups[group_index], preferred_element_type=jnp.float32)
        partial_term = lax.optimization_barrier(partial_term.astype(jnp.bfloat16)).astype(jnp.float32)
        return (summed + partial_term, None)
    projected, _ = lax.scan(add_group, jnp.zeros((TOKENS, D), jnp.float32), jnp.arange(N_HEAD))
    return (projected * gate[None, :]).astype(jnp.bfloat16)
```

```python
import math

import jax
import jax.numpy as jnp
from jax import lax
from jax.experimental import pallas as pl
from jax.experimental.pallas import tpu as pltpu
from jax.sharding import PartitionSpec as P

HD = 128
REACH = 3


NEG_FILL = -1e30


def shifted(block, axis, distance):
    devices = range(lax.axis_size(axis))
    route = [(i - distance, i) for i in devices if i - distance in devices]
    return lax.ppermute(block, axis, route)


def tile_scores(query_tiles, key_tiles):
    scores = jnp.einsum(
        "aqhd,bkhd->abhqk", query_tiles, key_tiles, preferred_element_type=jnp.float32
    )
    return scores * (1.0 / math.sqrt(query_tiles.shape[-1]))


def local(queries, keys, values, kv_list, kv_count, out_weight, gate):
    tiles_here = kv_list.shape[0]
    tile_rows = queries.shape[0] // tiles_here
    width = queries.shape[1]
    heads_here = width // HD
    query_tiles = queries.reshape(tiles_here, tile_rows, heads_here, HD)
    kv_pair = jnp.stack([keys, values])
    position = lax.axis_index(("seq", "sub"))
    places = lax.axis_size(("seq", "sub"))
    blocks = [(position, kv_pair)]
    for offset in range(1, REACH + 1):
        for heading in (offset, -offset):
            blocks.append((position - heading, shifted(kv_pair, ("seq", "sub"), heading)))
    live_slots = jnp.arange(kv_list.shape[1])[None, :] < kv_count[:, None]

    def included(anchor):
        inside = (anchor >= 0) & (anchor < places)
        neighbour = anchor * tiles_here + jnp.arange(tiles_here, dtype=jnp.int32)
        hits = (kv_list[:, :, None] == neighbour[None, None, :]) & live_slots[:, :, None]
        return jnp.any(hits, axis=1) & inside

    peak = jnp.full((tiles_here, heads_here, tile_rows), NEG_FILL, jnp.float32)
    for anchor, fetched in blocks:
        block_mask = included(anchor)
        block_key_tiles = fetched[0].reshape(tiles_here, tile_rows, heads_here, HD)
        scores = jnp.where(
            block_mask[:, :, None, None, None], tile_scores(query_tiles, block_key_tiles), NEG_FILL
        )
        peak = jnp.maximum(peak, jnp.max(scores, axis=(1, 4)))
    state = (
        jnp.zeros((tiles_here, tile_rows, heads_here, HD), jnp.float32),
        jnp.zeros((tiles_here, heads_here, tile_rows), jnp.float32),
    )
    for anchor, fetched in blocks:
        mask = included(anchor)
        key_tiles = fetched[0].reshape(tiles_here, tile_rows, heads_here, HD)
        value_tiles = fetched[1].reshape(tiles_here, tile_rows, heads_here, HD)
        compute_accum, compute_total = state
        compute_scores = jnp.where(
            mask[:, :, None, None, None], tile_scores(query_tiles, key_tiles), NEG_FILL
        )
        weights = jnp.exp(compute_scores - peak[:, None, :, :, None])
        compute_total = compute_total + jnp.sum(weights, axis=(1, 4))
        compute_accum = compute_accum + jnp.einsum(
            "abhqk,bkhd->aqhd",
            weights.astype(jnp.bfloat16),
            value_tiles,
            preferred_element_type=jnp.float32,
        )
        state = (compute_accum, compute_total)
    accum, total = state
    attention = (
        (accum / jnp.transpose(total, (0, 2, 1))[:, :, :, None])
        .reshape(tiles_here * tile_rows, width)
        .astype(jnp.bfloat16)
    )
    summed = lax.psum_scatter(
        lax.dot_general(
            out_weight, attention, (((0,), (1,)), ((), ())), preferred_element_type=jnp.float32
        ).astype(jnp.bfloat16),
        "head",
        scatter_dimension=0,
        tiled=True,
    ).astype(jnp.float32)
    return (jnp.transpose(summed) * gate[None, :]).astype(jnp.bfloat16)


HEADS_PER_CHUNK = 2
AHEAD = 3
WEIGHT_PIECES = 3
MESH = pl.DeviceIdType.MESH


def fused_kernel(
    q_hbm, k_hbm, v_hbm, list_ref, count_ref, w_hbm, gate_ref, out_ref,
    q_buf, kv, att, w_own, w_rem, acc,
    kv_in, q_in, w_in, kv_send, kv_recv, att_send, att_recv, w_send, w_recv,
):
    chunks = kv.shape[1]
    cols = kv.shape[4]
    width = q_buf.shape[1]
    quarter = w_rem.shape[2]
    piece_rows = width // WEIGHT_PIECES
    y, z = lax.axis_index("groups"), lax.axis_index("seq")
    x, s = lax.axis_index("head"), lax.axis_index("sub")
    z_size = lax.axis_size("seq")
    has_low, has_high = z > 0, z < z_size - 1
    core, across, other = {"sub": 1 - s}, {"head": 1 - x}, {"groups": 1 - y}
    low, high = {"seq": z - 1}, {"seq": z + 1}

    def lanes(start, size):
        return pl.ds(pl.multiple_of(start, HD), size)

    def own_in(c, which):
        src = (k_hbm, v_hbm)[which]
        return pltpu.make_async_copy(
            src.at[:, lanes(c * cols, cols)], kv.at[0, c, which], kv_in.at[c, which]
        )

    def kv_copy(way, src_slot, dst_slot, c, device):
        return pltpu.make_async_remote_copy(
            src_ref=kv.at[src_slot, c], dst_ref=kv.at[dst_slot, c],
            send_sem=kv_send.at[way, c], recv_sem=kv_recv.at[dst_slot, c],
            device_id=device, device_id_type=MESH,
        )

    def up(c):
        return kv_copy(0, 0, 2, c, high)

    def down(c):
        return kv_copy(1, 0, 4, c, low)

    def side(c):
        return kv_copy(2, 0, 1, c, core)

    def side_low(c):
        return kv_copy(3, 2, 3, c, core)

    def side_high(c):
        return kv_copy(4, 4, 5, c, core)

    def arrived(slot, c):
        kv_copy(2, 0, slot, c, core).wait_recv()

    def att_copy(c):
        piece = lanes(c * cols, cols)
        return pltpu.make_async_remote_copy(
            src_ref=att.at[0, :, piece], dst_ref=att.at[1, :, piece],
            send_sem=att_send.at[c], recv_sem=att_recv.at[c],
            device_id=across, device_id_type=MESH,
        )

    mine, theirs = y * 2 + s, (1 - y) * 2 + s

    def w_across(p):
        rows = pl.ds(p * piece_rows, piece_rows)
        return pltpu.make_async_remote_copy(
            src_ref=w_hbm.at[rows, lanes((1 - x) * width + mine * quarter, quarter)],
            dst_ref=w_rem.at[mine, rows], send_sem=w_send.at[0, p], recv_sem=w_recv.at[0, p],
            device_id=across, device_id_type=MESH,
        )

    def w_forward(way, place, p, device):
        rows = pl.ds(p * piece_rows, piece_rows)
        return pltpu.make_async_remote_copy(
            src_ref=w_rem.at[place, rows], dst_ref=w_rem.at[place, rows],
            send_sem=w_send.at[way, p], recv_sem=w_recv.at[way, p],
            device_id=device, device_id_type=MESH,
        )

    def w_other(p):
        return w_forward(1, mine, p, other)

    def w_side(p):
        return w_forward(2, mine, p, core)

    def w_side_other(p):
        return w_forward(3, theirs, p, core)

    q_copy = pltpu.make_async_copy(q_hbm, q_buf, q_in)
    w_copy = pltpu.make_async_copy(w_hbm.at[:, lanes(x * width, width)], w_own, w_in)

    @pl.loop(0, chunks)
    def _(c):
        own_in(c, 0).start()
        own_in(c, 1).start()

    q_copy.start()

    barrier = pltpu.get_barrier_semaphore()
    for device in (core, across, other):
        pl.semaphore_signal(barrier, inc=1, device_id=device, device_id_type=MESH)

    @pl.when(has_low)
    def _():
        pl.semaphore_signal(barrier, inc=1, device_id=low, device_id_type=MESH)

    @pl.when(has_high)
    def _():
        pl.semaphore_signal(barrier, inc=1, device_id=high, device_id_type=MESH)

    pl.semaphore_wait(barrier, 3 + (z > 0).astype(jnp.int32) + (z < z_size - 1).astype(jnp.int32))

    def send_along(c):
        @pl.when(has_high)
        def _():
            up(c).start()

        @pl.when(has_low)
        def _():
            down(c).start()

    @pl.loop(0, chunks)
    def _(c):
        own_in(c, 0).wait()
        own_in(c, 1).wait()

        @pl.when(c < AHEAD)
        def _():
            send_along(c)

    @pl.loop(0, WEIGHT_PIECES)
    def _(p):
        w_across(p).start()

    @pl.loop(0, chunks)
    def _(c):
        side(c).start()

    w_copy.start()

    @pl.when(jnp.logical_not(has_low))
    def _():
        @pl.loop(0, chunks)
        def _(c):
            kv[2, c] = jnp.zeros(kv.shape[2:], kv.dtype)
            kv[3, c] = jnp.zeros(kv.shape[2:], kv.dtype)

    @pl.when(jnp.logical_not(has_high))
    def _():
        @pl.loop(0, chunks)
        def _(c):
            kv[4, c] = jnp.zeros(kv.shape[2:], kv.dtype)
            kv[5, c] = jnp.zeros(kv.shape[2:], kv.dtype)

    tiles = [
        z * 2 + s, z * 2 + 1 - s,
        z * 2 - 2 + s, z * 2 - 1 - s,
        z * 2 + 2 + s, z * 2 + 3 - s,
    ]
    count = count_ref[0]
    biases = []
    for slot, tile in enumerate(tiles):
        bias = jnp.float32(NEG_FILL)
        for j in range(list_ref.shape[1]):
            hit = (list_ref[0, j] == tile) & (j < count)
            bias = jnp.where(hit, jnp.float32(0.0), bias)
        if slot in (2, 3):
            bias = jnp.where(has_low, bias, jnp.float32(NEG_FILL))
        if slot in (4, 5):
            bias = jnp.where(has_high, bias, jnp.float32(NEG_FILL))
        biases.append(bias)
    factor = (1.0 / math.sqrt(HD)) * math.log2(math.e)
    q_copy.wait()

    @pl.loop(0, chunks)
    def _(c):
        @pl.when(has_low)
        def _():
            arrived(2, c)
            side_low(c).start()

        @pl.when(has_high)
        def _():
            arrived(4, c)
            side_high(c).start()

        @pl.when(c + AHEAD < chunks)
        def _():
            send_along(c + AHEAD)

        @pl.when((c >= 1) & (c < 1 + WEIGHT_PIECES))
        def _():
            w_across(c - 1).wait_recv()
            w_other(c - 1).start()
            w_side(c - 1).start()

        @pl.when((c >= 3) & (c < 3 + WEIGHT_PIECES))
        def _():
            w_other(c - 3).wait_recv()
            w_side_other(c - 3).start()

        arrived(1, c)

        @pl.when(has_low)
        def _():
            arrived(3, c)

        @pl.when(has_high)
        def _():
            arrived(5, c)

        for h in range(cols // HD):
            head = pl.ds(h * HD, HD)
            place = lanes(c * cols + h * HD, HD)
            query = q_buf[:, place]
            scores = [
                lax.dot_general(
                    query, kv[t, c, 0, :, head], (((1,), (1,)), ((), ())),
                    preferred_element_type=jnp.float32,
                )
                for t in range(6)
            ]
            peak = None
            for t in range(6):
                top = jnp.max(scores[t], axis=1, keepdims=True) * factor + biases[t]
                peak = top if peak is None else jnp.maximum(peak, top)
            total, mixed = None, None
            for t in range(6):
                weights = jnp.exp2(scores[t] * factor - (peak - biases[t]))
                part = jnp.sum(weights, axis=1, keepdims=True)
                term = jnp.dot(
                    weights.astype(jnp.bfloat16), kv[t, c, 1, :, head],
                    preferred_element_type=jnp.float32,
                )
                total = part if total is None else total + part
                mixed = term if mixed is None else mixed + term
            att[0, :, place] = (mixed / total).astype(jnp.bfloat16)
        att_copy(c).start()

    w_copy.wait()
    for q in range(4):
        span = pl.ds(q * quarter, quarter)
        acc[:, span] = jnp.dot(att[0], w_own[:, span], preferred_element_type=jnp.float32)

    @pl.loop(0, WEIGHT_PIECES)
    def _(p):
        w_side(p).wait_recv()
        w_side_other(p).wait_recv()

    @pl.loop(0, chunks - 1)
    def _(c):
        att_copy(c).wait_recv()

    early = (chunks - 1) * cols
    for q in range(4):
        span = pl.ds(q * quarter, quarter)
        acc[:, span] += jnp.dot(
            att[1, :, :early], w_rem[q, :early, :], preferred_element_type=jnp.float32
        )
    att_copy(chunks - 1).wait_recv()
    for q in range(4):
        span = pl.ds(q * quarter, quarter)
        done = acc[:, span] + jnp.dot(
            att[1, :, early:], w_rem[q, early:, :], preferred_element_type=jnp.float32
        )
        out_ref[:, span] = (done * gate_ref[:, span]).astype(out_ref.dtype)

    @pl.loop(0, chunks)
    def _(c):
        side(c).wait_send()
        att_copy(c).wait_send()

        @pl.when(has_high)
        def _():
            up(c).wait_send()
            side_high(c).wait_send()

        @pl.when(has_low)
        def _():
            down(c).wait_send()
            side_low(c).wait_send()

    @pl.loop(0, WEIGHT_PIECES)
    def _(p):
        w_across(p).wait_send()
        w_other(p).wait_send()
        w_side(p).wait_send()
        w_side_other(p).wait_send()


def fused(queries, keys, values, kv_list, kv_count, out_weight, gate):
    rows, width = queries.shape
    cols = HEADS_PER_CHUNK * HD
    chunks = width // cols
    dma = pltpu.SemaphoreType.DMA
    anywhere = pl.BlockSpec(memory_space=pl.ANY)
    scalar = pl.BlockSpec(memory_space=pltpu.SMEM)
    vector = pl.BlockSpec(memory_space=pltpu.VMEM)
    return pl.pallas_call(
        fused_kernel,
        out_shape=jax.ShapeDtypeStruct((rows, width), jnp.bfloat16),
        in_specs=[anywhere, anywhere, anywhere, scalar, scalar, anywhere, vector],
        out_specs=vector,
        scratch_shapes=[
            pltpu.VMEM((rows, width), jnp.bfloat16),
            pltpu.VMEM((6, chunks, 2, rows, cols), jnp.bfloat16),
            pltpu.VMEM((2, rows, width), jnp.bfloat16),
            pltpu.VMEM((width, width), jnp.bfloat16),
            pltpu.VMEM((4, width, width // 4), jnp.bfloat16),
            pltpu.VMEM((rows, width), jnp.float32),
            dma((chunks, 2)),
            dma,
            dma,
            dma((5, chunks)),
            dma((6, chunks)),
            dma((chunks,)),
            dma((chunks,)),
            dma((4, WEIGHT_PIECES)),
            dma((4, WEIGHT_PIECES)),
        ],
        compiler_params=pltpu.CompilerParams(
            collective_id=0, has_side_effects=True, vmem_limit_bytes=56 * 1024 * 1024
        ),
    )(queries, keys, values, kv_list, kv_count, out_weight, gate.reshape(1, -1))


def solution(mesh):
    shape = mesh.shape
    paired = shape["head"] == 2 and shape["groups"] == 2 and shape["sub"] == 2

    def body(queries, keys, values, kv_list, kv_count, out_weight, gate):
        chosen = fused if paired and kv_list.shape[0] == 1 else local
        return chosen(queries, keys, values, kv_list, kv_count, out_weight, gate)

    return jax.shard_map(
        body,
        mesh=mesh,
        in_specs=(
            P(("groups", "seq", "sub"), "head"),
            P(("groups", "seq", "sub"), "head"),
            P(("groups", "seq", "sub"), "head"),
            P(("groups", "seq", "sub"), None),
            P(("groups", "seq", "sub")),
            P("head", None),
            P("head"),
        ),
        out_specs=P(("groups", "seq", "sub"), "head"),
        check_vma=False,
    )
```

```python
import math

import jax
import jax.numpy as jnp
from jax import lax
from jax.experimental import pallas as pl
from jax.experimental.pallas import tpu as pltpu
from jax.sharding import PartitionSpec as P

HD = 128
REACH = 3


NEG_FILL = -1e30


def shifted(block, axis, distance):
    devices = range(lax.axis_size(axis))
    route = [(i - distance, i) for i in devices if i - distance in devices]
    return lax.ppermute(block, axis, route)


def tile_scores(query_tiles, key_tiles):
    scores = jnp.einsum(
        "aqhd,bkhd->abhqk", query_tiles, key_tiles, preferred_element_type=jnp.float32
    )
    return scores * (1.0 / math.sqrt(query_tiles.shape[-1]))


def local(queries, keys, values, kv_list, kv_count, out_weight, gate):
    tiles_here = kv_list.shape[0]
    tile_rows = queries.shape[0] // tiles_here
    width = queries.shape[1]
    heads_here = width // HD
    query_tiles = queries.reshape(tiles_here, tile_rows, heads_here, HD)
    kv_pair = jnp.stack([keys, values])
    position = lax.axis_index(("seq", "sub"))
    places = lax.axis_size(("seq", "sub"))
    blocks = [(position, kv_pair)]
    for offset in range(1, REACH + 1):
        for heading in (offset, -offset):
            blocks.append((position - heading, shifted(kv_pair, ("seq", "sub"), heading)))
    live_slots = jnp.arange(kv_list.shape[1])[None, :] < kv_count[:, None]

    def included(anchor):
        inside = (anchor >= 0) & (anchor < places)
        neighbour = anchor * tiles_here + jnp.arange(tiles_here, dtype=jnp.int32)
        hits = (kv_list[:, :, None] == neighbour[None, None, :]) & live_slots[:, :, None]
        return jnp.any(hits, axis=1) & inside

    peak = jnp.full((tiles_here, heads_here, tile_rows), NEG_FILL, jnp.float32)
    for anchor, fetched in blocks:
        block_mask = included(anchor)
        block_key_tiles = fetched[0].reshape(tiles_here, tile_rows, heads_here, HD)
        scores = jnp.where(
            block_mask[:, :, None, None, None], tile_scores(query_tiles, block_key_tiles), NEG_FILL
        )
        peak = jnp.maximum(peak, jnp.max(scores, axis=(1, 4)))
    state = (
        jnp.zeros((tiles_here, tile_rows, heads_here, HD), jnp.float32),
        jnp.zeros((tiles_here, heads_here, tile_rows), jnp.float32),
    )
    for anchor, fetched in blocks:
        mask = included(anchor)
        key_tiles = fetched[0].reshape(tiles_here, tile_rows, heads_here, HD)
        value_tiles = fetched[1].reshape(tiles_here, tile_rows, heads_here, HD)
        compute_accum, compute_total = state
        compute_scores = jnp.where(
            mask[:, :, None, None, None], tile_scores(query_tiles, key_tiles), NEG_FILL
        )
        weights = jnp.exp(compute_scores - peak[:, None, :, :, None])
        compute_total = compute_total + jnp.sum(weights, axis=(1, 4))
        compute_accum = compute_accum + jnp.einsum(
            "abhqk,bkhd->aqhd",
            weights.astype(jnp.bfloat16),
            value_tiles,
            preferred_element_type=jnp.float32,
        )
        state = (compute_accum, compute_total)
    accum, total = state
    attention = (
        (accum / jnp.transpose(total, (0, 2, 1))[:, :, :, None])
        .reshape(tiles_here * tile_rows, width)
        .astype(jnp.bfloat16)
    )
    summed = lax.psum_scatter(
        lax.dot_general(
            out_weight, attention, (((0,), (1,)), ((), ())), preferred_element_type=jnp.float32
        ).astype(jnp.bfloat16),
        "head",
        scatter_dimension=0,
        tiled=True,
    ).astype(jnp.float32)
    return (jnp.transpose(summed) * gate[None, :]).astype(jnp.bfloat16)


HEADS_PER_CHUNK = 1
AHEAD = 3
WEIGHT_PIECES = 6
MESH = pl.DeviceIdType.MESH


def fused_kernel(
    q_hbm, k_hbm, v_hbm, list_ref, count_ref, w_hbm, gate_ref, out_ref,
    q_buf, kv, att, w_own, w_rem, acc,
    kv_in, q_in, w_in, kv_send, kv_recv, att_send, att_recv, w_send, w_recv,
):
    chunks = kv.shape[1]
    cols = kv.shape[4]
    width = q_buf.shape[1]
    quarter = w_rem.shape[2]
    piece_rows = width // WEIGHT_PIECES
    y, z = lax.axis_index("groups"), lax.axis_index("seq")
    x, s = lax.axis_index("head"), lax.axis_index("sub")
    z_size = lax.axis_size("seq")
    has_low, has_high = z > 0, z < z_size - 1
    core, across, other = {"sub": 1 - s}, {"head": 1 - x}, {"groups": 1 - y}
    low, high = {"seq": z - 1}, {"seq": z + 1}

    def lanes(start, size):
        return pl.ds(pl.multiple_of(start, HD), size)

    def own_in(c, which):
        src = (k_hbm, v_hbm)[which]
        return pltpu.make_async_copy(
            src.at[:, lanes(c * cols, cols)], kv.at[0, c, which], kv_in.at[c, which]
        )

    def kv_copy(way, src_slot, dst_slot, c, device):
        return pltpu.make_async_remote_copy(
            src_ref=kv.at[src_slot, c], dst_ref=kv.at[dst_slot, c],
            send_sem=kv_send.at[way, c], recv_sem=kv_recv.at[dst_slot, c],
            device_id=device, device_id_type=MESH,
        )

    def up(c):
        return kv_copy(0, 0, 2, c, high)

    def down(c):
        return kv_copy(1, 0, 4, c, low)

    def side(c):
        return kv_copy(2, 0, 1, c, core)

    def side_low(c):
        return kv_copy(3, 2, 3, c, core)

    def side_high(c):
        return kv_copy(4, 4, 5, c, core)

    def arrived(slot, c):
        kv_copy(2, 0, slot, c, core).wait_recv()

    def att_copy(c):
        piece = lanes(c * cols, cols)
        return pltpu.make_async_remote_copy(
            src_ref=att.at[0, :, piece], dst_ref=att.at[1, :, piece],
            send_sem=att_send.at[c], recv_sem=att_recv.at[c],
            device_id=across, device_id_type=MESH,
        )

    mine, theirs = y * 2 + s, (1 - y) * 2 + s

    def w_across(p):
        rows = pl.ds(p * piece_rows, piece_rows)
        return pltpu.make_async_remote_copy(
            src_ref=w_hbm.at[rows, lanes((1 - x) * width + mine * quarter, quarter)],
            dst_ref=w_rem.at[mine, rows], send_sem=w_send.at[0, p], recv_sem=w_recv.at[0, p],
            device_id=across, device_id_type=MESH,
        )

    def w_forward(way, place, p, device):
        rows = pl.ds(p * piece_rows, piece_rows)
        return pltpu.make_async_remote_copy(
            src_ref=w_rem.at[place, rows], dst_ref=w_rem.at[place, rows],
            send_sem=w_send.at[way, p], recv_sem=w_recv.at[way, p],
            device_id=device, device_id_type=MESH,
        )

    def w_other(p):
        return w_forward(1, mine, p, other)

    def w_side(p):
        return w_forward(2, mine, p, core)

    def w_side_other(p):
        return w_forward(3, theirs, p, core)

    q_copy = pltpu.make_async_copy(q_hbm, q_buf, q_in)
    w_copy = pltpu.make_async_copy(w_hbm.at[:, lanes(x * width, width)], w_own, w_in)

    @pl.loop(0, chunks)
    def _(c):
        own_in(c, 0).start()
        own_in(c, 1).start()

    q_copy.start()

    barrier = pltpu.get_barrier_semaphore()
    for device in (core, across, other):
        pl.semaphore_signal(barrier, inc=1, device_id=device, device_id_type=MESH)

    @pl.when(has_low)
    def _():
        pl.semaphore_signal(barrier, inc=1, device_id=low, device_id_type=MESH)

    @pl.when(has_high)
    def _():
        pl.semaphore_signal(barrier, inc=1, device_id=high, device_id_type=MESH)

    pl.semaphore_wait(barrier, 3 + (z > 0).astype(jnp.int32) + (z < z_size - 1).astype(jnp.int32))

    def send_along(c):
        @pl.when(has_high)
        def _():
            up(c).start()

        @pl.when(has_low)
        def _():
            down(c).start()

    @pl.loop(0, chunks)
    def _(c):
        own_in(c, 0).wait()
        own_in(c, 1).wait()

        @pl.when(c < AHEAD)
        def _():
            send_along(c)

    @pl.loop(0, WEIGHT_PIECES)
    def _(p):
        w_across(p).start()

    @pl.loop(0, chunks)
    def _(c):
        side(c).start()

    w_copy.start()

    @pl.when(jnp.logical_not(has_low))
    def _():
        @pl.loop(0, chunks)
        def _(c):
            kv[2, c] = jnp.zeros(kv.shape[2:], kv.dtype)
            kv[3, c] = jnp.zeros(kv.shape[2:], kv.dtype)

    @pl.when(jnp.logical_not(has_high))
    def _():
        @pl.loop(0, chunks)
        def _(c):
            kv[4, c] = jnp.zeros(kv.shape[2:], kv.dtype)
            kv[5, c] = jnp.zeros(kv.shape[2:], kv.dtype)

    tiles = [
        z * 2 + s, z * 2 + 1 - s,
        z * 2 - 2 + s, z * 2 - 1 - s,
        z * 2 + 2 + s, z * 2 + 3 - s,
    ]
    count = count_ref[0]
    biases = []
    for slot, tile in enumerate(tiles):
        bias = jnp.float32(NEG_FILL)
        for j in range(list_ref.shape[1]):
            hit = (list_ref[0, j] == tile) & (j < count)
            bias = jnp.where(hit, jnp.float32(0.0), bias)
        if slot in (2, 3):
            bias = jnp.where(has_low, bias, jnp.float32(NEG_FILL))
        if slot in (4, 5):
            bias = jnp.where(has_high, bias, jnp.float32(NEG_FILL))
        biases.append(bias)
    factor = (1.0 / math.sqrt(HD)) * math.log2(math.e)
    q_copy.wait()

    @pl.loop(0, chunks)
    def _(c):
        @pl.when(has_low)
        def _():
            arrived(2, c)
            side_low(c).start()

        @pl.when(has_high)
        def _():
            arrived(4, c)
            side_high(c).start()

        @pl.when(c + AHEAD < chunks)
        def _():
            send_along(c + AHEAD)

        @pl.when((c >= 3) & (c < 3 + WEIGHT_PIECES))
        def _():
            w_across(c - 3).wait_recv()
            w_other(c - 3).start()
            w_side(c - 3).start()

        @pl.when((c >= 6) & (c < 6 + WEIGHT_PIECES))
        def _():
            w_other(c - 6).wait_recv()
            w_side_other(c - 6).start()

        arrived(1, c)

        @pl.when(has_low)
        def _():
            arrived(3, c)

        @pl.when(has_high)
        def _():
            arrived(5, c)

        for h in range(cols // HD):
            head = pl.ds(h * HD, HD)
            place = lanes(c * cols + h * HD, HD)
            query = q_buf[:, place]
            scores = [
                lax.dot_general(
                    query, kv[t, c, 0, :, head], (((1,), (1,)), ((), ())),
                    preferred_element_type=jnp.float32,
                )
                for t in range(6)
            ]
            peak = None
            for t in range(6):
                top = jnp.max(scores[t], axis=1, keepdims=True) * factor + biases[t]
                peak = top if peak is None else jnp.maximum(peak, top)
            total, mixed = None, None
            for t in range(6):
                weights = jnp.exp2(scores[t] * factor - (peak - biases[t]))
                part = jnp.sum(weights, axis=1, keepdims=True)
                term = jnp.dot(
                    weights.astype(jnp.bfloat16), kv[t, c, 1, :, head],
                    preferred_element_type=jnp.float32,
                )
                total = part if total is None else total + part
                mixed = term if mixed is None else mixed + term
            att[0, :, place] = (mixed / total).astype(jnp.bfloat16)
        att_copy(c).start()

    w_copy.wait()
    for q in range(4):
        span = pl.ds(q * quarter, quarter)
        acc[:, span] = jnp.dot(att[0], w_own[:, span], preferred_element_type=jnp.float32)

    @pl.loop(0, WEIGHT_PIECES)
    def _(p):
        w_side(p).wait_recv()
        w_side_other(p).wait_recv()

    @pl.loop(0, chunks - 1)
    def _(c):
        att_copy(c).wait_recv()

    early = (chunks - 1) * cols
    for q in range(4):
        span = pl.ds(q * quarter, quarter)
        acc[:, span] += jnp.dot(
            att[1, :, :early], w_rem[q, :early, :], preferred_element_type=jnp.float32
        )
    att_copy(chunks - 1).wait_recv()
    for q in range(4):
        span = pl.ds(q * quarter, quarter)
        done = acc[:, span] + jnp.dot(
            att[1, :, early:], w_rem[q, early:, :], preferred_element_type=jnp.float32
        )
        out_ref[:, span] = (done * gate_ref[span][None, :]).astype(out_ref.dtype)

    @pl.loop(0, chunks)
    def _(c):
        side(c).wait_send()
        att_copy(c).wait_send()

        @pl.when(has_high)
        def _():
            up(c).wait_send()
            side_high(c).wait_send()

        @pl.when(has_low)
        def _():
            down(c).wait_send()
            side_low(c).wait_send()

    @pl.loop(0, WEIGHT_PIECES)
    def _(p):
        w_across(p).wait_send()
        w_other(p).wait_send()
        w_side(p).wait_send()
        w_side_other(p).wait_send()


def fused(queries, keys, values, kv_list, kv_count, out_weight, gate):
    rows, width = queries.shape
    cols = HEADS_PER_CHUNK * HD
    chunks = width // cols
    dma = pltpu.SemaphoreType.DMA
    anywhere = pl.BlockSpec(memory_space=pl.ANY)
    scalar = pl.BlockSpec(memory_space=pltpu.SMEM)
    vector = pl.BlockSpec(memory_space=pltpu.VMEM)
    return pl.pallas_call(
        fused_kernel,
        out_shape=jax.ShapeDtypeStruct((rows, width), jnp.bfloat16),
        in_specs=[anywhere, anywhere, anywhere, scalar, scalar, anywhere, vector],
        out_specs=vector,
        scratch_shapes=[
            pltpu.VMEM((rows, width), jnp.bfloat16),
            pltpu.VMEM((6, chunks, 2, rows, cols), jnp.bfloat16),
            pltpu.VMEM((2, rows, width), jnp.bfloat16),
            pltpu.VMEM((width, width), jnp.bfloat16),
            pltpu.VMEM((4, width, width // 4), jnp.bfloat16),
            pltpu.VMEM((rows, width), jnp.float32),
            dma((chunks, 2)),
            dma,
            dma,
            dma((5, chunks)),
            dma((6, chunks)),
            dma((chunks,)),
            dma((chunks,)),
            dma((4, WEIGHT_PIECES)),
            dma((4, WEIGHT_PIECES)),
        ],
        compiler_params=pltpu.CompilerParams(
            collective_id=0, has_side_effects=True, vmem_limit_bytes=56 * 1024 * 1024
        ),
    )(queries, keys, values, kv_list, kv_count, out_weight, gate)


def solution(mesh):
    shape = mesh.shape
    paired = shape["head"] == 2 and shape["groups"] == 2 and shape["sub"] == 2

    def body(queries, keys, values, kv_list, kv_count, out_weight, gate):
        chosen = fused if paired and kv_list.shape[0] == 1 else local
        return chosen(queries, keys, values, kv_list, kv_count, out_weight, gate)

    return jax.shard_map(
        body,
        mesh=mesh,
        in_specs=(
            P(("groups", "seq", "sub"), "head"),
            P(("groups", "seq", "sub"), "head"),
            P(("groups", "seq", "sub"), "head"),
            P(("groups", "seq", "sub"), None),
            P(("groups", "seq", "sub")),
            P("head", None),
            P("head"),
        ),
        out_specs=P(("groups", "seq", "sub"), "head"),
        check_vma=False,
    )
```

```python
import math

import jax
import jax.numpy as jnp
from jax import lax
from jax.experimental import pallas as pl
from jax.experimental.pallas import tpu as pltpu
from jax.sharding import PartitionSpec as P

HD = 128
REACH = 3


NEG_FILL = -1e30


def shifted(block, axis, distance):
    devices = range(lax.axis_size(axis))
    route = [(i - distance, i) for i in devices if i - distance in devices]
    return lax.ppermute(block, axis, route)


def tile_scores(query_tiles, key_tiles):
    scores = jnp.einsum(
        "aqhd,bkhd->abhqk", query_tiles, key_tiles, preferred_element_type=jnp.float32
    )
    return scores * (1.0 / math.sqrt(query_tiles.shape[-1]))


def local(queries, keys, values, kv_list, kv_count, out_weight, gate):
    tiles_here = kv_list.shape[0]
    tile_rows = queries.shape[0] // tiles_here
    width = queries.shape[1]
    heads_here = width // HD
    query_tiles = queries.reshape(tiles_here, tile_rows, heads_here, HD)
    kv_pair = jnp.stack([keys, values])
    position = lax.axis_index(("seq", "sub"))
    places = lax.axis_size(("seq", "sub"))
    blocks = [(position, kv_pair)]
    for offset in range(1, REACH + 1):
        for heading in (offset, -offset):
            blocks.append((position - heading, shifted(kv_pair, ("seq", "sub"), heading)))
    live_slots = jnp.arange(kv_list.shape[1])[None, :] < kv_count[:, None]

    def included(anchor):
        inside = (anchor >= 0) & (anchor < places)
        neighbour = anchor * tiles_here + jnp.arange(tiles_here, dtype=jnp.int32)
        hits = (kv_list[:, :, None] == neighbour[None, None, :]) & live_slots[:, :, None]
        return jnp.any(hits, axis=1) & inside

    peak = jnp.full((tiles_here, heads_here, tile_rows), NEG_FILL, jnp.float32)
    for anchor, fetched in blocks:
        block_mask = included(anchor)
        block_key_tiles = fetched[0].reshape(tiles_here, tile_rows, heads_here, HD)
        scores = jnp.where(
            block_mask[:, :, None, None, None], tile_scores(query_tiles, block_key_tiles), NEG_FILL
        )
        peak = jnp.maximum(peak, jnp.max(scores, axis=(1, 4)))
    state = (
        jnp.zeros((tiles_here, tile_rows, heads_here, HD), jnp.float32),
        jnp.zeros((tiles_here, heads_here, tile_rows), jnp.float32),
    )
    for anchor, fetched in blocks:
        mask = included(anchor)
        key_tiles = fetched[0].reshape(tiles_here, tile_rows, heads_here, HD)
        value_tiles = fetched[1].reshape(tiles_here, tile_rows, heads_here, HD)
        compute_accum, compute_total = state
        compute_scores = jnp.where(
            mask[:, :, None, None, None], tile_scores(query_tiles, key_tiles), NEG_FILL
        )
        weights = jnp.exp(compute_scores - peak[:, None, :, :, None])
        compute_total = compute_total + jnp.sum(weights, axis=(1, 4))
        compute_accum = compute_accum + jnp.einsum(
            "abhqk,bkhd->aqhd",
            weights.astype(jnp.bfloat16),
            value_tiles,
            preferred_element_type=jnp.float32,
        )
        state = (compute_accum, compute_total)
    accum, total = state
    attention = (
        (accum / jnp.transpose(total, (0, 2, 1))[:, :, :, None])
        .reshape(tiles_here * tile_rows, width)
        .astype(jnp.bfloat16)
    )
    summed = lax.psum_scatter(
        lax.dot_general(
            out_weight, attention, (((0,), (1,)), ((), ())), preferred_element_type=jnp.float32
        ).astype(jnp.bfloat16),
        "head",
        scatter_dimension=0,
        tiled=True,
    ).astype(jnp.float32)
    return (jnp.transpose(summed) * gate[None, :]).astype(jnp.bfloat16)


HEADS_PER_CHUNK = 1
AHEAD = 3
WEIGHT_PIECES = 6
MESH = pl.DeviceIdType.MESH


def fused_kernel(
    q_hbm, k_hbm, v_hbm, list_ref, count_ref, w_hbm, gate_ref, out_ref,
    q_buf, kv, att, w_own, w_rem, acc,
    kv_in, q_in, w_in, kv_send, kv_recv, att_send, att_recv, w_send, w_recv,
):
    chunks = kv.shape[1]
    cols = kv.shape[4]
    width = q_buf.shape[1]
    quarter = w_rem.shape[2]
    piece_rows = width // WEIGHT_PIECES
    y, z = lax.axis_index("groups"), lax.axis_index("seq")
    x, s = lax.axis_index("head"), lax.axis_index("sub")
    z_size = lax.axis_size("seq")
    has_low, has_high = z > 0, z < z_size - 1
    core, across, other = {"sub": 1 - s}, {"head": 1 - x}, {"groups": 1 - y}
    low, high = {"seq": z - 1}, {"seq": z + 1}

    def lanes(start, size):
        return pl.ds(pl.multiple_of(start, HD), size)

    def own_in(c, which):
        src = (k_hbm, v_hbm)[which]
        return pltpu.make_async_copy(
            src.at[:, lanes(c * cols, cols)], kv.at[0, c, which], kv_in.at[c, which]
        )

    def kv_copy(way, src_slot, dst_slot, c, device):
        return pltpu.make_async_remote_copy(
            src_ref=kv.at[src_slot, c], dst_ref=kv.at[dst_slot, c],
            send_sem=kv_send.at[way, c], recv_sem=kv_recv.at[dst_slot, c],
            device_id=device, device_id_type=MESH,
        )

    def up(c):
        return kv_copy(0, 0, 2, c, high)

    def down(c):
        return kv_copy(1, 0, 4, c, low)

    def side(c):
        return kv_copy(2, 0, 1, c, core)

    def side_low(c):
        return kv_copy(3, 2, 3, c, core)

    def side_high(c):
        return kv_copy(4, 4, 5, c, core)

    def arrived(slot, c):
        kv_copy(2, 0, slot, c, core).wait_recv()

    def att_copy(c):
        piece = lanes(c * cols, cols)
        return pltpu.make_async_remote_copy(
            src_ref=att.at[0, :, piece], dst_ref=att.at[1, :, piece],
            send_sem=att_send.at[c], recv_sem=att_recv.at[c],
            device_id=across, device_id_type=MESH,
        )

    mine, theirs = y * 2 + s, (1 - y) * 2 + s

    def w_across(p):
        rows = pl.ds(p * piece_rows, piece_rows)
        return pltpu.make_async_remote_copy(
            src_ref=w_hbm.at[rows, lanes((1 - x) * width + mine * quarter, quarter)],
            dst_ref=w_rem.at[mine, rows], send_sem=w_send.at[0, p], recv_sem=w_recv.at[0, p],
            device_id=across, device_id_type=MESH,
        )

    def w_forward(way, place, p, device):
        rows = pl.ds(p * piece_rows, piece_rows)
        return pltpu.make_async_remote_copy(
            src_ref=w_rem.at[place, rows], dst_ref=w_rem.at[place, rows],
            send_sem=w_send.at[way, p], recv_sem=w_recv.at[way, p],
            device_id=device, device_id_type=MESH,
        )

    def w_other(p):
        return w_forward(1, mine, p, other)

    def w_side(p):
        return w_forward(2, mine, p, core)

    def w_side_other(p):
        return w_forward(3, theirs, p, core)

    q_copy = pltpu.make_async_copy(q_hbm, q_buf, q_in)
    w_copy = pltpu.make_async_copy(w_hbm.at[:, lanes(x * width, width)], w_own, w_in)

    @pl.loop(0, chunks)
    def _(c):
        own_in(c, 0).start()
        own_in(c, 1).start()

    q_copy.start()

    barrier = pltpu.get_barrier_semaphore()
    for device in (core, across, other):
        pl.semaphore_signal(barrier, inc=1, device_id=device, device_id_type=MESH)

    @pl.when(has_low)
    def _():
        pl.semaphore_signal(barrier, inc=1, device_id=low, device_id_type=MESH)

    @pl.when(has_high)
    def _():
        pl.semaphore_signal(barrier, inc=1, device_id=high, device_id_type=MESH)

    pl.semaphore_wait(barrier, 3 + (z > 0).astype(jnp.int32) + (z < z_size - 1).astype(jnp.int32))

    def send_along(c):
        @pl.when(has_high)
        def _():
            up(c).start()

        @pl.when(has_low)
        def _():
            down(c).start()

    @pl.loop(0, chunks)
    def _(c):
        own_in(c, 0).wait()
        own_in(c, 1).wait()

        @pl.when(c < AHEAD)
        def _():
            send_along(c)

    @pl.loop(0, WEIGHT_PIECES)
    def _(p):
        w_across(p).start()

    @pl.loop(0, chunks)
    def _(c):
        side(c).start()

    w_copy.start()

    @pl.when(jnp.logical_not(has_low))
    def _():
        @pl.loop(0, chunks)
        def _(c):
            kv[2, c] = jnp.zeros(kv.shape[2:], kv.dtype)
            kv[3, c] = jnp.zeros(kv.shape[2:], kv.dtype)

    @pl.when(jnp.logical_not(has_high))
    def _():
        @pl.loop(0, chunks)
        def _(c):
            kv[4, c] = jnp.zeros(kv.shape[2:], kv.dtype)
            kv[5, c] = jnp.zeros(kv.shape[2:], kv.dtype)

    tiles = [
        z * 2 + s, z * 2 + 1 - s,
        z * 2 - 2 + s, z * 2 - 1 - s,
        z * 2 + 2 + s, z * 2 + 3 - s,
    ]
    count = count_ref[0]
    biases = []
    for slot, tile in enumerate(tiles):
        bias = jnp.float32(NEG_FILL)
        for j in range(list_ref.shape[1]):
            hit = (list_ref[0, j] == tile) & (j < count)
            bias = jnp.where(hit, jnp.float32(0.0), bias)
        if slot in (2, 3):
            bias = jnp.where(has_low, bias, jnp.float32(NEG_FILL))
        if slot in (4, 5):
            bias = jnp.where(has_high, bias, jnp.float32(NEG_FILL))
        biases.append(bias)
    factor = (1.0 / math.sqrt(HD)) * math.log2(math.e)
    q_copy.wait()
    half = chunks // 2 * cols

    @pl.loop(0, chunks)
    def _(c):
        @pl.when(has_low)
        def _():
            arrived(2, c)
            side_low(c).start()

        @pl.when(has_high)
        def _():
            arrived(4, c)
            side_high(c).start()

        @pl.when(c + AHEAD < chunks)
        def _():
            send_along(c + AHEAD)

        @pl.when((c >= 3) & (c < 3 + WEIGHT_PIECES))
        def _():
            w_across(c - 3).wait_recv()
            w_other(c - 3).start()
            w_side(c - 3).start()

        @pl.when((c >= 6) & (c < 6 + WEIGHT_PIECES))
        def _():
            w_other(c - 6).wait_recv()
            w_side_other(c - 6).start()

        @pl.when(c == chunks // 2)
        def _():
            w_copy.wait()
            for q in range(4):
                span = pl.ds(q * quarter, quarter)
                acc[:, span] = jnp.dot(
                    att[0, :, :half], w_own[:half, span], preferred_element_type=jnp.float32
                )

        arrived(1, c)

        @pl.when(has_low)
        def _():
            arrived(3, c)

        @pl.when(has_high)
        def _():
            arrived(5, c)

        for h in range(cols // HD):
            head = pl.ds(h * HD, HD)
            place = lanes(c * cols + h * HD, HD)
            query = q_buf[:, place]
            scores = [
                lax.dot_general(
                    query, kv[t, c, 0, :, head], (((1,), (1,)), ((), ())),
                    preferred_element_type=jnp.float32,
                )
                for t in range(6)
            ]
            peak = None
            for t in range(6):
                top = jnp.max(scores[t], axis=1, keepdims=True) * factor + biases[t]
                peak = top if peak is None else jnp.maximum(peak, top)
            total, mixed = None, None
            for t in range(6):
                weights = jnp.exp2(scores[t] * factor - (peak - biases[t]))
                part = jnp.sum(weights, axis=1, keepdims=True)
                term = jnp.dot(
                    weights.astype(jnp.bfloat16), kv[t, c, 1, :, head],
                    preferred_element_type=jnp.float32,
                )
                total = part if total is None else total + part
                mixed = term if mixed is None else mixed + term
            att[0, :, place] = (mixed / total).astype(jnp.bfloat16)
        att_copy(c).start()

    for q in range(4):
        span = pl.ds(q * quarter, quarter)
        acc[:, span] += jnp.dot(
            att[0, :, half:], w_own[half:, span], preferred_element_type=jnp.float32
        )

    @pl.loop(0, WEIGHT_PIECES)
    def _(p):
        w_side(p).wait_recv()
        w_side_other(p).wait_recv()

    @pl.loop(0, chunks - 1)
    def _(c):
        att_copy(c).wait_recv()

    early = (chunks - 1) * cols
    for q in range(4):
        span = pl.ds(q * quarter, quarter)
        acc[:, span] += jnp.dot(
            att[1, :, :early], w_rem[q, :early, :], preferred_element_type=jnp.float32
        )
    att_copy(chunks - 1).wait_recv()
    for q in range(4):
        span = pl.ds(q * quarter, quarter)
        done = acc[:, span] + jnp.dot(
            att[1, :, early:], w_rem[q, early:, :], preferred_element_type=jnp.float32
        )
        out_ref[:, span] = (done * gate_ref[span][None, :]).astype(out_ref.dtype)

    @pl.loop(0, chunks)
    def _(c):
        side(c).wait_send()
        att_copy(c).wait_send()

        @pl.when(has_high)
        def _():
            up(c).wait_send()
            side_high(c).wait_send()

        @pl.when(has_low)
        def _():
            down(c).wait_send()
            side_low(c).wait_send()

    @pl.loop(0, WEIGHT_PIECES)
    def _(p):
        w_across(p).wait_send()
        w_other(p).wait_send()
        w_side(p).wait_send()
        w_side_other(p).wait_send()


def fused(queries, keys, values, kv_list, kv_count, out_weight, gate):
    rows, width = queries.shape
    cols = HEADS_PER_CHUNK * HD
    chunks = width // cols
    dma = pltpu.SemaphoreType.DMA
    anywhere = pl.BlockSpec(memory_space=pl.ANY)
    scalar = pl.BlockSpec(memory_space=pltpu.SMEM)
    vector = pl.BlockSpec(memory_space=pltpu.VMEM)
    return pl.pallas_call(
        fused_kernel,
        out_shape=jax.ShapeDtypeStruct((rows, width), jnp.bfloat16),
        in_specs=[anywhere, anywhere, anywhere, scalar, scalar, anywhere, vector],
        out_specs=vector,
        scratch_shapes=[
            pltpu.VMEM((rows, width), jnp.bfloat16),
            pltpu.VMEM((6, chunks, 2, rows, cols), jnp.bfloat16),
            pltpu.VMEM((2, rows, width), jnp.bfloat16),
            pltpu.VMEM((width, width), jnp.bfloat16),
            pltpu.VMEM((4, width, width // 4), jnp.bfloat16),
            pltpu.VMEM((rows, width), jnp.float32),
            dma((chunks, 2)),
            dma,
            dma,
            dma((5, chunks)),
            dma((6, chunks)),
            dma((chunks,)),
            dma((chunks,)),
            dma((4, WEIGHT_PIECES)),
            dma((4, WEIGHT_PIECES)),
        ],
        compiler_params=pltpu.CompilerParams(
            collective_id=0, has_side_effects=True, vmem_limit_bytes=56 * 1024 * 1024
        ),
    )(queries, keys, values, kv_list, kv_count, out_weight, gate)


def solution(mesh):
    shape = mesh.shape
    paired = shape["head"] == 2 and shape["groups"] == 2 and shape["sub"] == 2

    def body(queries, keys, values, kv_list, kv_count, out_weight, gate):
        chosen = fused if paired and kv_list.shape[0] == 1 else local
        return chosen(queries, keys, values, kv_list, kv_count, out_weight, gate)

    return jax.shard_map(
        body,
        mesh=mesh,
        in_specs=(
            P(("groups", "seq", "sub"), "head"),
            P(("groups", "seq", "sub"), "head"),
            P(("groups", "seq", "sub"), "head"),
            P(("groups", "seq", "sub"), None),
            P(("groups", "seq", "sub")),
            P("head", None),
            P("head"),
        ),
        out_specs=P(("groups", "seq", "sub"), "head"),
        check_vma=False,
    )
```
